256 devices in a mesh: node: 32 (over y, z), local: 8 (over x, core).
Axes of the slice: x: 4, y: 4, z: 8, core: 2. Of those that a mesh axis runs over, the one named last changes fastest.
Arguments:
- tokens: bfloat16 [4096, 6144], P('node', 'local'), may hold values from -15 to 15
- weight_values: bfloat16 [6144, 6144], P('node', 'local'), may hold values from -5 to 5
- weight_scales: bfloat16 [192, 48], P('node', 'local'), may hold values from 0.0039978027 to 0.039794922
- out_cotangent: bfloat16 [4096, 6144], P('node', 'local'), may hold values from -15 to 15
Outputs:
- queries: bfloat16 [4096, 6144], P('node', 'local')
- token_grad: bfloat16 [4096, 6144], P('node', 'local')
- weight_grad: float32 [6144, 6144], P('node', 'local')
The draws below stay inside these ranges and needn't reach their ends.
All inputs are finite; a program needn't handle non-finite values.
Results may differ from the reference program's by a relative error of at most 0.017.
Values may be sent and summed in bfloat16 or wider, within the bound.
No kernel may reach another device: no remote copies, remote signals or barrier semaphores. Data moves between devices by JAX's collectives and lax.ppermute only.
A program may use at most 192 MiB of HBM per device.

```python
import math
import jax
import jax.numpy as jnp
from jax import lax

DIN = 6144
DOUT = 6144
BR = 32
BC = 128
TOK = 128
TOKENS = 4096
N_NODE = 32
N_LOCAL = 8


def feature_field(key, width, block):
    scale_key, noise_key = jax.random.split(key, 2)
    logs = jax.random.uniform(scale_key, (width // block,), jnp.float32, math.log(0.3), math.log(3.0))
    scale = jnp.repeat(jnp.exp(logs), block)
    mixed = jax.random.truncated_normal(noise_key, -5.0, 5.0, (TOKENS, width), jnp.float32)
    return (mixed * scale[None, :]).astype(jnp.bfloat16)


def draw_tokens(key, part):
    key = jax.random.fold_in(key, 11)
    return feature_field(key, DIN, BR)


def draw_out_cotangent(key, part):
    key = jax.random.fold_in(key, 12)
    return feature_field(key, DOUT, BC)


def block_levels(rng, dims, cuts, low, high):
    factor_of, own = 1.0, jax.random.fold_in(rng, 6)
    for position, shards_of in cuts:
        steps = jnp.exp(jax.random.uniform(jax.random.fold_in(own, position), (shards_of,), jnp.float32, low / len(cuts), high / len(cuts)))
        factor_of = factor_of * jnp.repeat(steps, dims[position] // shards_of).reshape([-1 if axis == position else 1 for axis in range(len(dims))])
    return factor_of


def gaussian(key, extent, scale, reach, cuts=(), kind=jnp.bfloat16):
    array = scale * jax.random.normal(key, extent, jnp.float32)
    if cuts:
        array = array * block_levels(key, extent, cuts, -0.22, 0.18)
    return jnp.clip(array, -reach, reach).astype(kind)


def setup_inputs(seed: int = 0) -> dict:
    keys = jax.random.split(jax.random.key(seed), 5)
    tokens = draw_tokens(jax.random.fold_in(keys[4], 71), 0)
    weight_values = gaussian(keys[1], (DIN, DOUT), 1.0, 5.0, ((0, 32), (1, 8)))
    weight_scales = jnp.clip(jnp.exp(math.log(0.039794922) - 2.2979944 * jax.random.uniform(keys[2], (DIN // BR, DOUT // BC), jnp.float32) ** block_levels(keys[2], (DIN // BR, DOUT // BC), ((0, 32), (1, 8)), -0.2, 0.2)), 0.0039978027, 0.039794922).astype(jnp.bfloat16)
    out_cotangent = draw_out_cotangent(jax.random.fold_in(keys[4], 71), 0)
    return {"tokens": tokens, "weight_values": weight_values, "weight_scales": weight_scales, "out_cotangent": out_cotangent}


level_top = 2.0

def spread(scales, rows, cols):
    wide = jnp.repeat(scales.astype(jnp.float32), rows, axis=-2)
    return jnp.repeat(wide, cols, axis=-1)

def quantize(partial_value):
    height, width = partial_value.shape
    blocks = partial_value.reshape(height // BR, BR, width // BC, BC)
    power = lax.optimization_barrier(jnp.mean(blocks * blocks, axis=(1, 3)))
    scale = jnp.sqrt(power + 1e-06).astype(jnp.bfloat16)
    ratio = partial_value / spread(scale, BR, BC)
    levels = jnp.clip(ratio, -level_top, level_top).astype(jnp.bfloat16)
    return (levels, scale)

def reference(tokens, weight_values, weight_scales, out_cotangent):
    weights = (weight_values.astype(jnp.float32) * spread(weight_scales, BR, BC)).astype(jnp.bfloat16)
    queries = jnp.dot(tokens, weights, preferred_element_type=jnp.float32).astype(jnp.bfloat16)
    slab_width = DOUT // N_LOCAL

    def slab_step(index, total):
        start = (index * slab_width).astype(jnp.int32)
        cots = lax.dynamic_slice_in_dim(out_cotangent, start, slab_width, 1)
        cols = lax.dynamic_slice_in_dim(weights, start, slab_width, 1)
        slab_grad = jnp.dot(cots, cols.T, preferred_element_type=jnp.float32).astype(jnp.bfloat16)
        return total + slab_grad.astype(jnp.float32)
    token_total = lax.fori_loop(0, N_LOCAL, slab_step, jnp.zeros((TOKENS, DIN), jnp.float32))
    token_grad = token_total.astype(jnp.bfloat16)
    factor = jnp.float32(1.0 / math.sqrt(TOKENS))

    def step(total, index):
        start = (index * TOK).astype(jnp.int32)
        rows = lax.dynamic_slice_in_dim(tokens, start, TOK, 0)
        cots = lax.dynamic_slice_in_dim(out_cotangent, start, TOK, 0)
        partial_value = lax.dot_general(rows, cots, (((0,), (0,)), ((), ())), preferred_element_type=jnp.float32) * factor
        levels, scale = quantize(partial_value)
        return (total + levels.astype(jnp.float32) * spread(scale, BR, BC), None)
    weight_grad, _ = lax.scan(step, jnp.zeros((DIN, DOUT), jnp.float32), jnp.arange(N_NODE, dtype=jnp.int32))
    return (queries, token_grad, weight_grad)
```

```python
import functools

import jax
import jax.numpy as jnp
from jax import lax
from jax.experimental import pallas as pl
from jax.experimental.pallas import tpu as pltpu
from jax.sharding import Mesh, PartitionSpec as P

BR = 32
BC = 128
TOP = 2.0
GROUPS_PER_STEP = 4
SPLIT = 112


def spread(scales, rows, cols):
    wide = jnp.repeat(scales.astype(jnp.float32), rows, axis=-2)
    return jnp.repeat(wide, cols, axis=-1)


def shift(a, axis, step):
    n = lax.axis_size(axis)
    return lax.ppermute(a, axis, [(i, (i + step) % n) for i in range(n)])


def ring(own, axis):
    n = lax.axis_size(axis)
    got = [None] * n
    got[0] = up = down = own
    for step in range(1, n // 2):
        up, down = shift(up, axis, 1), shift(down, axis, -1)
        got[n - step], got[step] = up, down
    half = own.shape[0] // 2
    got[n // 2] = jnp.concatenate([shift(up[:half], axis, 1), shift(down[half:], axis, -1)])
    return got


def turn(a, by, axis):
    return lax.dynamic_slice_in_dim(jnp.concatenate([a, a], axis), by, a.shape[axis], axis)


def gather_local(own):
    x, core = lax.axis_index("x"), lax.axis_index("core")
    mine = jnp.stack(ring(own, "x"))
    other = shift(mine, "core", 1)
    pair = jnp.stack([jnp.where(core == 0, mine, other), jnp.where(core == 0, other, mine)], axis=1)
    return turn(pair, (4 - x) % 4, 0)


def grad_kernel(x_ref, d_ref, o_ref, p_ref):
    @pl.when(pl.program_id(0) == 0)
    def _():
        o_ref[...] = jnp.zeros_like(o_ref)

    rows, width = o_ref.shape
    nb = rows // BR
    for s in range(x_ref.shape[0]):
        p_ref[s] = jnp.dot(x_ref[s], d_ref[s], preferred_element_type=jnp.float32)
        p = p_ref[s].reshape(nb, BR, width)
        col = jnp.sum(p * p, axis=1)
        tot = jnp.concatenate(
            [
                jnp.broadcast_to(jnp.sum(col[:, j : j + BC], axis=1, keepdims=True), (nb, BC))
                for j in range(0, width, BC)
            ],
            axis=1,
        )
        scale = jnp.sqrt(tot * 2.0**-24 + 1e-6).astype(jnp.bfloat16).astype(jnp.float32)
        inv = 0.015625 / scale
        for i in range(nb):
            part = p_ref[s, i * BR : (i + 1) * BR, :]
            level = jnp.clip(part * inv[i : i + 1, :], -TOP, TOP).astype(jnp.bfloat16)
            o_ref[i * BR : (i + 1) * BR, :] += level.astype(jnp.float32) * scale[i : i + 1, :]


def weight_gradient(xs, ds):
    groups, rows, tok = xs.shape
    cols = ds.shape[2]
    per = GROUPS_PER_STEP
    return pl.pallas_call(
        grad_kernel,
        grid=(groups // per,),
        in_specs=[
            pl.BlockSpec((per, rows, tok), lambda g: (g, 0, 0)),
            pl.BlockSpec((per, tok, cols), lambda g: (g, 0, 0)),
        ],
        out_specs=pl.BlockSpec((rows, cols), lambda g: (0, 0)),
        out_shape=jax.ShapeDtypeStruct((rows, cols), jnp.float32),
        scratch_shapes=[pltpu.VMEM((per, rows, cols), jnp.float32)],
        compiler_params=pltpu.CompilerParams(vmem_limit_bytes=32 * 2**20),
        cost_estimate=pl.CostEstimate(
            flops=2 * groups * rows * tok * cols, bytes_accessed=9 * 2**20, transcendentals=0
        ),
    )(xs, ds)


def dot0(a, b):
    return lax.dot_general(a, b, (((0,), (0,)), ((), ())), preferred_element_type=jnp.float32)


def local(tokens, weight_values, weight_scales, out_cotangent):
    y, z = lax.axis_index("y"), lax.axis_index("z")
    l = lax.axis_index(("x", "core"))
    ny, nz = lax.axis_size("y"), lax.axis_size("z")
    nodes, nloc = ny * nz, lax.axis_size(("x", "core"))
    rows, width = weight_values.shape
    tok = tokens.shape[0]

    got_cot = lax.all_gather(out_cotangent, ("y", "z"), axis=0)
    weights = (weight_values.astype(jnp.float32) * spread(weight_scales, BR, BC)).astype(jnp.bfloat16)

    with jax.named_scope("gather_tokens"):
        full = gather_local(tokens.T).reshape(nodes, rows, tok)
    with jax.named_scope("token_slab"):
        piece = full.reshape(nodes, nloc, rows // nloc, tok)
        piece = lax.dynamic_index_in_dim(piece, l, 1, keepdims=False)
        piece = lax.all_to_all(piece, ("y", "z"), split_axis=0, concat_axis=0, tiled=True)
        slab = gather_local(piece).reshape(nloc, nodes, rows // nloc, tok)
        slab = slab.transpose(1, 0, 2, 3).reshape(nodes, rows, tok)

    with jax.named_scope("gather_weights"):
        first = jnp.stack(ring(weights[:SPLIT], "z"))
        second = jnp.stack(ring(weights[SPLIT:], "y"))
        w_a = ring(first, "y")
        w_b = ring(second, "z")

    x_rel = turn(turn(full.reshape(ny, nz, rows, tok), y, 0), z, 1)
    queries = jnp.zeros((tok, width), jnp.float32)
    dx_a, dx_b = [], []
    for d, w in enumerate(w_a):
        flat = w.reshape(nz * SPLIT, width)
        queries += dot0(x_rel[d, :, :SPLIT].reshape(nz * SPLIT, tok), flat)
        dx = jnp.dot(flat, out_cotangent.T, preferred_element_type=jnp.float32)
        dx_a.append(dx.astype(jnp.bfloat16).reshape(nz, SPLIT, tok))
    for d, w in enumerate(w_b):
        flat = w.reshape(ny * (rows - SPLIT), width)
        queries += dot0(x_rel[:, d, SPLIT:].reshape(ny * (rows - SPLIT), tok), flat)
        dx = jnp.dot(flat, out_cotangent.T, preferred_element_type=jnp.float32)
        dx_b.append(dx.astype(jnp.bfloat16).reshape(ny, rows - SPLIT, tok))
    queries = queries.astype(jnp.bfloat16)
    with jax.named_scope("token_grad"):
        dx = jnp.concatenate([jnp.stack(dx_a), jnp.stack(dx_b, axis=1)], axis=2)
        dx = turn(turn(dx, (ny - y) % ny, 0), (nz - z) % nz, 1).reshape(nloc, -1, tok)
        dx = lax.all_to_all(dx, ("x", "core"), split_axis=0, concat_axis=0, tiled=True)
        token_grad = jnp.sum(dx.astype(jnp.float32), axis=0).astype(jnp.bfloat16).T

    weight_grad = weight_gradient(slab, got_cot)
    return (queries, token_grad, weight_grad)


def solution(mesh):
    cube = Mesh(mesh.devices.reshape(4, 8, 4, 2), ("y", "z", "x", "core"))
    spec = P(("y", "z"), ("x", "core"))
    return jax.shard_map(
        local, mesh=cube, in_specs=(spec,) * 4, out_specs=(spec,) * 3, check_vma=False
    )
```

```python
import functools

import jax
import jax.numpy as jnp
from jax import lax
from jax.experimental import pallas as pl
from jax.experimental.pallas import tpu as pltpu
from jax.sharding import Mesh, PartitionSpec as P

BR = 32
BC = 128
TOP = 2.0
GROUPS_PER_STEP = 4
SPLIT = 96


def spread(scales, rows, cols):
    wide = jnp.repeat(scales.astype(jnp.float32), rows, axis=-2)
    return jnp.repeat(wide, cols, axis=-1)


def shift(a, axis, step):
    n = lax.axis_size(axis)
    return lax.ppermute(a, axis, [(i, (i + step) % n) for i in range(n)])


def both(up, down, axis):
    return shift(up, axis, 1), shift(down, axis, -1)


def halves(up, down):
    half = up.shape[0] // 2
    return up[:half], down[half:]


def together(*arrays):
    return lax.optimization_barrier(arrays)


def after(a, *others):
    return lax.optimization_barrier((a,) + others)[0]


def swap_local(a):
    return lax.all_to_all(a, ("x", "core"), split_axis=0, concat_axis=0, tiled=True)


def gather_local(own):
    n = lax.axis_size(("x", "core"))
    return swap_local(jnp.broadcast_to(own, (n,) + own.shape))


def grad_kernel(x_ref, d_ref, o_ref, p_ref):
    @pl.when(pl.program_id(0) == 0)
    def _():
        o_ref[...] = jnp.zeros_like(o_ref)

    rows, width = o_ref.shape
    nb = rows // BR
    for s in range(x_ref.shape[0]):
        p_ref[s] = jnp.dot(x_ref[s], d_ref[s], preferred_element_type=jnp.float32)
        p = p_ref[s].reshape(nb, BR, width)
        col = jnp.sum(p * p, axis=1)
        tot = jnp.concatenate(
            [
                jnp.broadcast_to(jnp.sum(col[:, j : j + BC], axis=1, keepdims=True), (nb, BC))
                for j in range(0, width, BC)
            ],
            axis=1,
        )
        scale = jnp.sqrt(tot * 2.0**-24 + 1e-6).astype(jnp.bfloat16).astype(jnp.float32)
        inv = 0.015625 / scale
        for i in range(nb):
            part = p_ref[s, i * BR : (i + 1) * BR, :]
            level = jnp.clip(part * inv[i : i + 1, :], -TOP, TOP).astype(jnp.bfloat16)
            o_ref[i * BR : (i + 1) * BR, :] += level.astype(jnp.float32) * scale[i : i + 1, :]


def weight_gradient(xs, ds):
    groups, rows, tok = xs.shape
    cols = ds.shape[2]
    per = GROUPS_PER_STEP
    return pl.pallas_call(
        grad_kernel,
        grid=(groups // per,),
        in_specs=[
            pl.BlockSpec((per, rows, tok), lambda g: (g, 0, 0)),
            pl.BlockSpec((per, tok, cols), lambda g: (g, 0, 0)),
        ],
        out_specs=pl.BlockSpec((rows, cols), lambda g: (0, 0)),
        out_shape=jax.ShapeDtypeStruct((rows, cols), jnp.float32),
        scratch_shapes=[pltpu.VMEM((per, rows, cols), jnp.float32)],
        compiler_params=pltpu.CompilerParams(vmem_limit_bytes=56 * 2**20),
        cost_estimate=pl.CostEstimate(
            flops=8 * 2 * groups * rows * tok * cols, bytes_accessed=9 * 2**20, transcendentals=0
        ),
    )(xs, ds)


def product_kernel(plan, pos_ref, x_ref, d_ref, q_in, dx_in, *refs):
    w_refs, (q_out, dx_out, xs) = refs[: len(plan)], refs[len(plan) :]
    ny, nz = x_ref.shape[:2]
    y, z = pos_ref[0], pos_ref[1]
    total = jnp.zeros(q_out.shape, jnp.float32) if q_in is None else q_in[...]
    if dx_in is not None:
        dx_out[...] = dx_in[...]
    for (kind, first, at), w_ref in zip(plan, w_refs):
        n, rows, width = w_ref.shape
        places = []
        for k in range(n):
            dy, dz = (first, at[k]) if kind == "a" else (at[k], first)
            place = (lax.rem(y + dy, ny), lax.rem(z + dz, nz), pl.ds(0 if kind == "a" else SPLIT, rows))
            xs[k * rows : (k + 1) * rows, :] = x_ref[place]
            places.append(place)
        w = w_ref[...].reshape(n * rows, width)
        total += lax.dot_general(
            xs[: n * rows, :], w, (((0,), (0,)), ((), ())), preferred_element_type=jnp.float32
        )
        terms = lax.dot_general(
            w, d_ref[...], (((1,), (1,)), ((), ())), preferred_element_type=jnp.float32
        ).astype(jnp.bfloat16)
        for k, place in enumerate(places):
            dx_out[place] = terms[k * rows : (k + 1) * rows, :]
    q_out[...] = total.astype(q_out.dtype)


def products(pos, x, d, pieces, before, out_type):
    plan = [(kind, first, at) for kind, first, at, _ in pieces]
    arrays = [w for *_, w in pieces]
    tok, width = d.shape
    vmem = pl.BlockSpec(memory_space=pltpu.VMEM)
    if before is None:
        body = lambda p, x, d, *refs: product_kernel(plan, p, x, d, None, None, *refs)
        before = ()
    else:
        body = functools.partial(product_kernel, plan)
    amount = sum(w.size for w in arrays)
    return pl.pallas_call(
        body,
        in_specs=[pl.BlockSpec(memory_space=pltpu.SMEM)] + [vmem] * (2 + len(before) + len(arrays)),
        out_specs=[vmem, vmem],
        out_shape=[
            jax.ShapeDtypeStruct((tok, width), out_type),
            jax.ShapeDtypeStruct(x.shape, jnp.bfloat16),
        ],
        scratch_shapes=[pltpu.VMEM((8 * SPLIT, tok), jnp.bfloat16)],
        compiler_params=pltpu.CompilerParams(vmem_limit_bytes=40 * 2**20),
        cost_estimate=pl.CostEstimate(
            flops=8 * 4 * tok * amount, bytes_accessed=2 * amount + 2**22, transcendentals=0
        ),
    )(pos, x, d, *before, *arrays)


def scatter_local(terms):
    x, core, n = lax.axis_index("x"), lax.axis_index("core"), lax.axis_size("x")
    terms = terms.reshape((n, 2) + terms.shape[1:])
    mine = lax.dynamic_index_in_dim(terms, core, 1, keepdims=False)
    got = shift(lax.dynamic_index_in_dim(terms, 1 - core, 1, keepdims=False), "core", 1)
    pair = (mine.astype(jnp.float32) + got.astype(jnp.float32)).astype(jnp.bfloat16)
    parts = [lax.dynamic_index_in_dim(pair, (x + d) % n, 0, keepdims=False) for d in range(n)]
    return [parts[0]] + [shift(parts[d], "x", d) for d in range(1, n)]


def local(tokens, weight_values, weight_scales, out_cotangent):
    y, z = lax.axis_index("y"), lax.axis_index("z")
    ny, nz = lax.axis_size("y"), lax.axis_size("z")
    nodes, nloc = ny * nz, lax.axis_size(("x", "core"))
    rows, width = weight_values.shape
    tok = tokens.shape[0]
    sub = rows // nloc

    tokens = tokens.T
    full = lax.all_gather(tokens, ("x", "core"), axis=0).reshape(ny, nz, rows, tok)
    weights = (weight_values.astype(jnp.float32) * spread(weight_scales, BR, BC)).astype(jnp.bfloat16)
    a, b = weights[:SPLIT], weights[SPLIT:]

    piece = tokens.reshape(nodes // nloc, nloc, sub, tok).transpose(1, 0, 2, 3)
    piece = swap_local(piece).reshape(nodes, sub, tok)
    a1, b1 = both(a, a, "z"), both(b, b, "y")
    a1u, a1d, b1u, b1d, out_cotangent = together(*a1, *b1, out_cotangent)
    got_cot = lax.all_gather(out_cotangent, ("y", "z"), axis=0)
    a2, b2 = both(a1u, a1d, "z"), both(*halves(b1u, b1d), "y")
    a3 = shift(a1u, "z", 2), shift(a1d, "z", -2)
    *a2, a3u, a3d, b2u, b2d, piece = together(*a2, *a3, *b2, piece)
    second = jnp.stack([b, b1d, jnp.concatenate([b2u, b2d]), b1u])
    near = jnp.stack([a, a1d, a2[0], a1u])
    c1 = both(second, second, "z")
    n1 = both(near, near, "y")
    a4 = shift(a3u, "z", 1)
    piece = lax.all_to_all(piece, ("y", "z"), split_axis=0, concat_axis=0, tiled=True)
    a4, c1u, c1d, n1u, n1d, piece = together(a4, *c1, *n1, piece)
    far = jnp.stack([a2[1], a3d, a4, a3u])
    f1 = both(far, far, "y")
    c2 = both(c1u, c1d, "z")
    c2u, c2d, f1u, f1d, piece = together(*c2, *f1, piece)
    c3 = both(c2u, c2d, "z")
    last = both(n1u, f1d, "y")
    slab = gather_local(piece)

    pos = jnp.stack([y, z])
    near_at, far_at, turn = (0, 1, nz - 2, nz - 1), (2, 3, 4, 5), tuple(range(ny))
    part = [("a", 0, near_at, near), ("a", 3, near_at, n1u), ("a", 1, near_at, n1d), ("a", 0, far_at, far)]
    part += [("a", 3, far_at, f1u), ("a", 1, far_at, f1d), ("b", 0, turn, second)]
    part += [("b", 7, turn, c1u), ("b", 1, turn, c1d), ("b", 6, turn, c2u), ("b", 2, turn, c2d)]
    part = products(pos, full, out_cotangent, part, None, jnp.float32)
    c3u, c3d, last_n, last_f, slab, *part = together(*c3, *last, slab, *part)
    slab = slab.transpose(1, 0, 2, 3).reshape(nodes, rows, tok)
    c4 = both(*halves(c3u, c3d), "z")
    more = [("a", 2, near_at, last_n), ("a", 2, far_at, last_f), ("b", 5, turn, c3u), ("b", 3, turn, c3d)]
    part = products(pos, full, out_cotangent, more, part, jnp.float32)
    late = [("b", 4, turn[: ny // 2], c4[0]), ("b", 4, turn[ny // 2 :], c4[1])]
    queries, dx = products(pos, full, out_cotangent, late, part, jnp.bfloat16)
    dx = scatter_local(dx.reshape(nloc, -1, tok))
    weight_grad = weight_gradient(slab, got_cot)
    *dx, weight_grad = together(*dx, weight_grad)
    token_grad = sum(d.astype(jnp.float32) for d in dx).astype(jnp.bfloat16).T
    return (queries, token_grad, weight_grad)


def solution(mesh):
    cube = Mesh(mesh.devices.reshape(4, 8, 4, 2), ("y", "z", "x", "core"))
    spec = P(("y", "z"), ("x", "core"))
    return jax.shard_map(
        local, mesh=cube, in_specs=(spec,) * 4, out_specs=(spec,) * 3, check_vma=False
    )
```

```python
import functools

import jax
import jax.numpy as jnp
from jax import lax
from jax.experimental import pallas as pl
from jax.experimental.pallas import tpu as pltpu
from jax.sharding import Mesh, PartitionSpec as P

BR = 32
BC = 128
TOP = 2.0
STEP = 2


def spread(scales, rows, cols):
    wide = jnp.repeat(scales.astype(jnp.float32), rows, axis=-2)
    return jnp.repeat(wide, cols, axis=-1)


def shift(a, axis, step):
    n = lax.axis_size(axis)
    return lax.ppermute(a, axis, [(i, (i + step) % n) for i in range(n)])


def together(*arrays):
    return lax.optimization_barrier(arrays)


def after(a, *others):
    return lax.optimization_barrier((a,) + others)[0]


def swap_local(a):
    return lax.all_to_all(a, ("x", "core"), split_axis=0, concat_axis=0, tiled=True)


def gather_local(own):
    n = lax.axis_size(("x", "core"))
    return swap_local(jnp.broadcast_to(own, (n,) + own.shape))


def grad_kernel(x_ref, g_ref, o_ref, p_ref):
    @pl.when(pl.program_id(0) == 0)
    def _():
        o_ref[...] = jnp.zeros_like(o_ref)

    ny, rows, width = o_ref.shape
    nb = rows // BR
    d = g_ref[0, rows:, :]
    for k in range(ny):
        p_ref[k] = jnp.dot(x_ref[0, k], d, preferred_element_type=jnp.float32)
        p = p_ref[k].reshape(nb, BR, width)
        col = jnp.sum(p * p, axis=1)
        tot = jnp.concatenate(
            [
                jnp.broadcast_to(jnp.sum(col[:, j : j + BC], axis=1, keepdims=True), (nb, BC))
                for j in range(0, width, BC)
            ],
            axis=1,
        )
        scale = jnp.sqrt(tot * 2.0**-24 + 1e-6).astype(jnp.bfloat16).astype(jnp.float32)
        inv = 0.015625 / scale
        for i in range(nb):
            part = p_ref[k, i * BR : (i + 1) * BR, :]
            level = jnp.clip(part * inv[i : i + 1, :], -TOP, TOP).astype(jnp.bfloat16)
            o_ref[k, i * BR : (i + 1) * BR, :] += level.astype(jnp.float32) * scale[i : i + 1, :]


def weight_gradient(xs, got):
    groups, ny, rows, tok = xs.shape
    cols = got.shape[2]
    return pl.pallas_call(
        grad_kernel,
        grid=(groups,),
        in_specs=[
            pl.BlockSpec((1, ny, rows, tok), lambda g: (g, 0, 0, 0)),
            pl.BlockSpec((1, rows + tok, cols), lambda g: (g, 0, 0)),
        ],
        out_specs=pl.BlockSpec((ny, rows, cols), lambda g: (0, 0, 0)),
        out_shape=jax.ShapeDtypeStruct((ny, rows, cols), jnp.float32),
        scratch_shapes=[pltpu.VMEM((ny, rows, cols), jnp.float32)],
        compiler_params=pltpu.CompilerParams(vmem_limit_bytes=48 * 2**20),
        cost_estimate=pl.CostEstimate(
            flops=8 * 2 * groups * ny * rows * tok * cols, bytes_accessed=2**23, transcendentals=0
        ),
    )(xs, got)


def product_kernel(x_ref, g_ref, d_ref, q_ref, dx_ref, acc):
    ny, n, rows, tok = x_ref.shape
    width = d_ref.shape[2]

    @pl.when(pl.program_id(0) == 0)
    def _():
        acc[...] = jnp.zeros_like(acc)

    w = g_ref[:, :rows, :].reshape(n * rows, width)
    for k in range(ny):
        x = x_ref[k].reshape(n * rows, tok)
        acc[k] += lax.dot_general(
            x, w, (((0,), (0,)), ((), ())), preferred_element_type=jnp.float32
        )
        terms = lax.dot_general(
            w, d_ref[k], (((1,), (1,)), ((), ())), preferred_element_type=jnp.float32
        )
        dx_ref[k] = terms.astype(jnp.bfloat16).reshape(n, rows, tok)

    @pl.when(pl.program_id(0) == pl.num_programs(0) - 1)
    def _():
        q_ref[...] = acc[...].astype(q_ref.dtype)


def products(x, got, d):
    ny, nz, rows, tok = x.shape
    width = d.shape[2]
    return pl.pallas_call(
        product_kernel,
        grid=(nz // STEP,),
        in_specs=[
            pl.BlockSpec((ny, STEP, rows, tok), lambda i: (0, i, 0, 0)),
            pl.BlockSpec((STEP, rows + tok, width), lambda i: (i, 0, 0)),
            pl.BlockSpec((ny, tok, width), lambda i: (0, 0, 0)),
        ],
        out_specs=[
            pl.BlockSpec((ny, tok, width), lambda i: (0, 0, 0)),
            pl.BlockSpec((ny, STEP, rows, tok), lambda i: (0, i, 0, 0)),
        ],
        out_shape=[
            jax.ShapeDtypeStruct((ny, tok, width), jnp.bfloat16),
            jax.ShapeDtypeStruct(x.shape, jnp.bfloat16),
        ],
        scratch_shapes=[pltpu.VMEM((ny, tok, width), jnp.float32)],
        compiler_params=pltpu.CompilerParams(vmem_limit_bytes=48 * 2**20),
        cost_estimate=pl.CostEstimate(
            flops=8 * 4 * ny * nz * rows * width * tok, bytes_accessed=2**23, transcendentals=0
        ),
    )(x, got, d)


def exchange(blocks, axis):
    n, me = lax.axis_size(axis), lax.axis_index(axis)
    parts = [lax.dynamic_index_in_dim(blocks, (me + d) % n, 0, keepdims=False) for d in range(n)]
    return [parts[0]] + [shift(parts[d], axis, d) for d in range(1, n)]


def total(parts):
    return sum(p.astype(jnp.float32) for p in parts).astype(jnp.bfloat16)


def swap_places(a):
    n = lax.axis_size("x")
    return lax.ppermute(a, ("y", "x"), [(i * n + j, j * n + i) for i in range(n) for j in range(n)])


def scatter_local(terms):
    core = lax.axis_index("core")
    mine = lax.dynamic_index_in_dim(terms, core, 1, keepdims=False)
    got = shift(lax.dynamic_index_in_dim(terms, 1 - core, 1, keepdims=False), "core", 1)
    return total(exchange(total([mine, got]), "x"))


def local(tokens, weight_values, weight_scales, out_cotangent):
    core = lax.axis_index("core")
    ny, nz = lax.axis_size("y"), lax.axis_size("z")
    rows, width = weight_values.shape
    tok = tokens.shape[0]
    half = rows // 2

    weights = (weight_values.astype(jnp.float32) * spread(weight_scales, BR, BC)).astype(jnp.bfloat16)
    got = lax.all_gather(jnp.concatenate([weights, out_cotangent]), "z", axis=0)
    cots = lax.all_gather(out_cotangent, "y", axis=0)

    tokens = tokens.T
    with jax.named_scope("token_slab"):
        parts = tokens.reshape(nz // 2, 2, half, tok)
        mine = lax.dynamic_index_in_dim(parts, core, 1, keepdims=False)
        other = shift(lax.dynamic_index_in_dim(parts, 1 - core, 1, keepdims=False), "core", 1)
        piece = jnp.where(core == 0, jnp.stack([mine, other]), jnp.stack([other, mine]))
        piece = piece.reshape(nz, half, tok)
        piece = lax.all_to_all(piece, "z", split_axis=0, concat_axis=0, tiled=True)
        slab = gather_local(piece).transpose(1, 0, 2, 3).reshape(nz, ny, rows, tok)
    with jax.named_scope("token_rows"):
        full = gather_local(swap_places(tokens)).reshape(ny, nz, rows, tok)

    partial_grad = weight_gradient(slab, got)
    weight_grad = lax.psum_scatter(partial_grad, "y", scatter_dimension=0, tiled=False)
    part, dx = products(after(full, partial_grad), got, cots)
    queries = total(exchange(part, "y"))
    dx = scatter_local(dx.reshape(lax.axis_size("x"), 2, -1, tok))
    token_grad = swap_places(dx).T
    return (queries, token_grad, weight_grad)


def solution(mesh):
    cube = Mesh(mesh.devices.reshape(4, 8, 4, 2), ("y", "z", "x", "core"))
    spec = P(("y", "z"), ("x", "core"))
    return jax.shard_map(
        local, mesh=cube, in_specs=(spec,) * 4, out_specs=(spec,) * 3, check_vma=False
    )
```

```python
import functools

import jax
import jax.numpy as jnp
from jax import lax
from jax.experimental import pallas as pl
from jax.experimental.pallas import tpu as pltpu
from jax.sharding import Mesh, PartitionSpec as P

BR = 32
BC = 128
TOP = 2.0
STEP = 2


def spread(scales, rows, cols):
    wide = jnp.repeat(scales.astype(jnp.float32), rows, axis=-2)
    return jnp.repeat(wide, cols, axis=-1)


def shift(a, axis, step):
    n = lax.axis_size(axis)
    return lax.ppermute(a, axis, [(i, (i + step) % n) for i in range(n)])


def together(*arrays):
    return lax.optimization_barrier(arrays)


def after(a, *others):
    return lax.optimization_barrier((a,) + others)[0]


def swap_local(a):
    return lax.all_to_all(a, ("x", "core"), split_axis=0, concat_axis=0, tiled=True)


def gather_local(own):
    n = lax.axis_size(("x", "core"))
    return swap_local(jnp.broadcast_to(own, (n,) + own.shape))


def grad_kernel(x_ref, d_ref, o_ref, acc, p_ref):
    @pl.when(pl.program_id(0) == 0)
    def _():
        acc[...] = jnp.zeros_like(acc)

    nz, rows, width = o_ref.shape
    nb = rows // BR
    for k in range(nz):
        p_ref[k] = jnp.dot(x_ref[0, k], d_ref[0], preferred_element_type=jnp.float32)
        p = p_ref[k].reshape(nb, BR, width)
        col = jnp.sum(p * p, axis=1)
        tot = jnp.concatenate(
            [
                jnp.broadcast_to(jnp.sum(col[:, j : j + BC], axis=1, keepdims=True), (nb, BC))
                for j in range(0, width, BC)
            ],
            axis=1,
        )
        scale = jnp.sqrt(tot * 2.0**-24 + 1e-6).astype(jnp.bfloat16).astype(jnp.float32)
        inv = 0.015625 / scale
        for i in range(nb):
            part = p_ref[k, i * BR : (i + 1) * BR, :]
            level = jnp.clip(part * inv[i : i + 1, :], -TOP, TOP).astype(jnp.bfloat16)
            acc[k, i * BR : (i + 1) * BR, :] += level.astype(jnp.float32) * scale[i : i + 1, :]

    @pl.when(pl.program_id(0) == pl.num_programs(0) - 1)
    def _():
        o_ref[...] = acc[...].astype(o_ref.dtype)


def weight_gradient(xs, cots):
    groups, nz, rows, tok = xs.shape
    cols = cots.shape[2]
    return pl.pallas_call(
        grad_kernel,
        grid=(groups,),
        in_specs=[
            pl.BlockSpec((1, nz, rows, tok), lambda g: (g, 0, 0, 0)),
            pl.BlockSpec((1, tok, cols), lambda g: (g, 0, 0)),
        ],
        out_specs=pl.BlockSpec((nz, rows, cols), lambda g: (0, 0, 0)),
        out_shape=jax.ShapeDtypeStruct((nz, rows, cols), jnp.bfloat16),
        scratch_shapes=[pltpu.VMEM((nz, rows, cols), jnp.float32)] * 2,
        compiler_params=pltpu.CompilerParams(vmem_limit_bytes=48 * 2**20),
        cost_estimate=pl.CostEstimate(
            flops=8 * 2 * groups * nz * rows * tok * cols, bytes_accessed=2**23, transcendentals=0
        ),
    )(xs, cots)


def product_kernel(x_ref, g_ref, d_ref, q_ref, dx_ref, acc):
    ny, n, rows, tok = x_ref.shape
    width = d_ref.shape[2]

    @pl.when(pl.program_id(0) == 0)
    def _():
        acc[...] = jnp.zeros_like(acc)

    w = g_ref[...].reshape(n * rows, width)
    for k in range(ny):
        x = x_ref[k].reshape(n * rows, tok)
        acc[k] += lax.dot_general(
            x, w, (((0,), (0,)), ((), ())), preferred_element_type=jnp.float32
        )
        terms = lax.dot_general(
            w, d_ref[k], (((1,), (1,)), ((), ())), preferred_element_type=jnp.float32
        )
        dx_ref[k] = terms.astype(jnp.bfloat16).reshape(n, rows, tok)

    @pl.when(pl.program_id(0) == pl.num_programs(0) - 1)
    def _():
        q_ref[...] = acc[...].astype(q_ref.dtype)


def products(x, got, d):
    ny, nz, rows, tok = x.shape
    width = d.shape[2]
    return pl.pallas_call(
        product_kernel,
        grid=(nz // STEP,),
        in_specs=[
            pl.BlockSpec((ny, STEP, rows, tok), lambda i: (0, i, 0, 0)),
            pl.BlockSpec((STEP, rows, width), lambda i: (i, 0, 0)),
            pl.BlockSpec((ny, tok, width), lambda i: (0, 0, 0)),
        ],
        out_specs=[
            pl.BlockSpec((ny, tok, width), lambda i: (0, 0, 0)),
            pl.BlockSpec((ny, STEP, rows, tok), lambda i: (0, i, 0, 0)),
        ],
        out_shape=[
            jax.ShapeDtypeStruct((ny, tok, width), jnp.bfloat16),
            jax.ShapeDtypeStruct(x.shape, jnp.bfloat16),
        ],
        scratch_shapes=[pltpu.VMEM((ny, tok, width), jnp.float32)],
        compiler_params=pltpu.CompilerParams(vmem_limit_bytes=48 * 2**20),
        cost_estimate=pl.CostEstimate(
            flops=8 * 4 * ny * nz * rows * width * tok, bytes_accessed=2**23, transcendentals=0
        ),
    )(x, got, d)


def exchange(blocks, axis):
    n, me = lax.axis_size(axis), lax.axis_index(axis)
    parts = [lax.dynamic_index_in_dim(blocks, (me + d) % n, 0, keepdims=False) for d in range(n)]
    return [parts[0]] + [shift(parts[d], axis, d) for d in range(1, n)]


def total(parts):
    return sum(p.astype(jnp.float32) for p in parts).astype(jnp.bfloat16)


def swap_places(a):
    n = lax.axis_size("x")
    return lax.ppermute(a, ("y", "x"), [(i * n + j, j * n + i) for i in range(n) for j in range(n)])


def scatter_local(terms):
    core = lax.axis_index("core")
    mine = lax.dynamic_index_in_dim(terms, core, 1, keepdims=False)
    got = shift(lax.dynamic_index_in_dim(terms, 1 - core, 1, keepdims=False), "core", 1)
    return total(exchange(total([mine, got]), "x"))


def local(tokens, weight_values, weight_scales, out_cotangent):
    ny, nz = lax.axis_size("y"), lax.axis_size("z")
    rows = weight_values.shape[0]
    tok = tokens.shape[0]

    weights = (weight_values.astype(jnp.float32) * spread(weight_scales, BR, BC)).astype(jnp.bfloat16)
    weights = lax.all_gather(weights, "z", axis=0)
    cots = lax.all_gather(out_cotangent, "y", axis=0)
    full = gather_local(swap_places(tokens.T)).reshape(ny, nz, rows, tok)

    partial_grad = weight_gradient(full, cots)
    weight_grad = lax.psum_scatter(partial_grad, "z", scatter_dimension=0, tiled=False)
    weight_grad = weight_grad.astype(jnp.float32)
    weights = after(weights, partial_grad)
    part, dx = products(full, weights, cots)
    queries = total(exchange(part, "y"))
    dx = scatter_local(dx.reshape(lax.axis_size("x"), 2, -1, tok))
    token_grad = swap_places(dx).T
    return (queries, token_grad, weight_grad)


def solution(mesh):
    cube = Mesh(mesh.devices.reshape(4, 8, 4, 2), ("y", "z", "x", "core"))
    spec = P(("y", "z"), ("x", "core"))
    return jax.shard_map(
        local, mesh=cube, in_specs=(spec,) * 4, out_specs=(spec,) * 3, check_vma=False
    )
```

```python
import functools

import jax
import jax.numpy as jnp
from jax import lax
from jax.experimental import pallas as pl
from jax.experimental.pallas import tpu as pltpu
from jax.sharding import Mesh, PartitionSpec as P

BR = 32
BC = 128
TOP = 2.0
STEP = 2


def spread(scales, rows, cols):
    wide = jnp.repeat(scales.astype(jnp.float32), rows, axis=-2)
    return jnp.repeat(wide, cols, axis=-1)


def shift(a, axis, step):
    n = lax.axis_size(axis)
    return lax.ppermute(a, axis, [(i, (i + step) % n) for i in range(n)])


def together(*arrays):
    return lax.optimization_barrier(arrays)


def after(a, *others):
    return lax.optimization_barrier((a,) + others)[0]


def swap_local(a):
    return lax.all_to_all(a, ("x", "core"), split_axis=0, concat_axis=0, tiled=True)


def gather_local(own):
    n = lax.axis_size(("x", "core"))
    return swap_local(jnp.broadcast_to(own, (n,) + own.shape))


def grad_kernel(x_ref, d_ref, o_ref, acc, p_ref):
    @pl.when(pl.program_id(0) == 0)
    def _():
        acc[...] = jnp.zeros_like(acc)

    nz, rows, width = o_ref.shape
    nb = rows // BR
    for k in range(nz):
        p_ref[k] = jnp.dot(x_ref[0, k], d_ref[0], preferred_element_type=jnp.float32)
        p = p_ref[k].reshape(nb, BR, width)
        col = jnp.sum(p * p, axis=1)
        tot = jnp.concatenate(
            [
                jnp.broadcast_to(jnp.sum(col[:, j : j + BC], axis=1, keepdims=True), (nb, BC))
                for j in range(0, width, BC)
            ],
            axis=1,
        )
        scale = jnp.sqrt(tot * 2.0**-24 + 1e-6).astype(jnp.bfloat16).astype(jnp.float32)
        inv = 0.015625 / scale
        for i in range(nb):
            part = p_ref[k, i * BR : (i + 1) * BR, :]
            level = jnp.clip(part * inv[i : i + 1, :], -TOP, TOP).astype(jnp.bfloat16)
            acc[k, i * BR : (i + 1) * BR, :] += level.astype(jnp.float32) * scale[i : i + 1, :]

    @pl.when(pl.program_id(0) == pl.num_programs(0) - 1)
    def _():
        o_ref[...] = acc[...].astype(o_ref.dtype)


def weight_gradient(xs, cots):
    groups, nz, rows, tok = xs.shape
    cols = cots.shape[2]
    return pl.pallas_call(
        grad_kernel,
        grid=(groups,),
        in_specs=[
            pl.BlockSpec((1, nz, rows, tok), lambda g: (g, 0, 0, 0)),
            pl.BlockSpec((1, tok, cols), lambda g: (g, 0, 0)),
        ],
        out_specs=pl.BlockSpec((nz, rows, cols), lambda g: (0, 0, 0)),
        out_shape=jax.ShapeDtypeStruct((nz, rows, cols), jnp.bfloat16),
        scratch_shapes=[pltpu.VMEM((nz, rows, cols), jnp.float32)] * 2,
        compiler_params=pltpu.CompilerParams(vmem_limit_bytes=48 * 2**20),
        cost_estimate=pl.CostEstimate(
            flops=8 * 2 * groups * nz * rows * tok * cols, bytes_accessed=2**23, transcendentals=0
        ),
    )(xs, cots)


def product_kernel(x_ref, g_ref, d_ref, q_ref, dx_ref, acc):
    ny, n, rows, tok = x_ref.shape
    width = d_ref.shape[2]

    @pl.when(pl.program_id(0) == 0)
    def _():
        acc[...] = jnp.zeros_like(acc)

    w = g_ref[...].reshape(n * rows, width)
    for k in range(ny):
        x = x_ref[k].reshape(n * rows, tok)
        acc[k] += lax.dot_general(
            x, w, (((0,), (0,)), ((), ())), preferred_element_type=jnp.float32
        )
        terms = lax.dot_general(
            w, d_ref[k], (((1,), (1,)), ((), ())), preferred_element_type=jnp.float32
        )
        dx_ref[0, k] = terms.astype(jnp.bfloat16).reshape(n, rows, tok)

    @pl.when(pl.program_id(0) == pl.num_programs(0) - 1)
    def _():
        q_ref[...] = acc[...].astype(q_ref.dtype)


def products(x, got, d):
    ny, nz, rows, tok = x.shape
    width = d.shape[2]
    steps = nz // STEP // 2
    return pl.pallas_call(
        product_kernel,
        grid=(nz // STEP,),
        in_specs=[
            pl.BlockSpec((ny, STEP, rows, tok), lambda i: (0, i, 0, 0)),
            pl.BlockSpec((STEP, rows, width), lambda i: (i, 0, 0)),
            pl.BlockSpec((ny, tok, width), lambda i: (0, 0, 0)),
        ],
        out_specs=[
            pl.BlockSpec((ny, tok, width), lambda i: (0, 0, 0)),
            pl.BlockSpec((1, ny, STEP, rows, tok), lambda i: (i // steps, 0, i % steps, 0, 0)),
        ],
        out_shape=[
            jax.ShapeDtypeStruct((ny, tok, width), jnp.bfloat16),
            jax.ShapeDtypeStruct((2, ny, nz // 2, rows, tok), jnp.bfloat16),
        ],
        scratch_shapes=[pltpu.VMEM((ny, tok, width), jnp.float32)],
        compiler_params=pltpu.CompilerParams(vmem_limit_bytes=48 * 2**20),
        cost_estimate=pl.CostEstimate(
            flops=8 * 4 * ny * nz * rows * width * tok, bytes_accessed=2**23, transcendentals=0
        ),
    )(x, got, d)


def exchange(blocks, axis):
    return [blocks[0]] + [shift(blocks[d], axis, d) for d in range(1, len(blocks))]


def total(parts):
    return sum(p.astype(jnp.float32) for p in parts).astype(jnp.bfloat16)


def around(a, k):
    n = lax.axis_size("x")
    pairs = [(i * n + j, j * n + (i + k) % n) for i in range(n) for j in range(n)]
    return lax.ppermute(a, ("y", "x"), pairs)


def sum_cores(terms):
    core = lax.axis_index("core")
    mine = lax.dynamic_index_in_dim(terms, core, 0, keepdims=False)
    got = shift(lax.dynamic_index_in_dim(terms, 1 - core, 0, keepdims=False), "core", 1)
    return total([mine, got])


def scatter_plane(terms):
    x, y, n = lax.axis_index("x"), lax.axis_index("y"), lax.axis_size("x")
    pick = lambda a, i: lax.dynamic_index_in_dim(a, i % n, 0, keepdims=False)
    rows = jnp.stack(exchange([pick(terms, x - y - d) for d in range(n)], "y"))
    return total(exchange([pick(rows, y - x - d) for d in range(n)], "x"))


def local(tokens, weight_values, weight_scales, out_cotangent):
    x, y = lax.axis_index("x"), lax.axis_index("y")
    ny, nz = lax.axis_size("y"), lax.axis_size("z")
    rows = weight_values.shape[0]
    tok = tokens.shape[0]

    weights = (weight_values.astype(jnp.float32) * spread(weight_scales, BR, BC)).astype(jnp.bfloat16)
    weights = lax.all_gather(weights, "z", axis=0)
    tokens = tokens.T
    mine = [around(tokens, k) for k in range(ny)]
    cots = [out_cotangent] + [shift(out_cotangent, "y", -d) for d in range(1, ny)]
    *mine, c1, c2, c3 = together(*mine, *cots[1:])
    cots = jnp.stack([out_cotangent, c1, c2, c3])
    cots = jnp.stack([lax.dynamic_index_in_dim(cots, (x - k - y) % ny, 0, keepdims=False) for k in range(ny)])
    mine = jnp.stack(mine)
    other = shift(mine, "core", 1)
    first = lax.axis_index("core") == 0
    full = jnp.stack([jnp.where(first, mine, other), jnp.where(first, other, mine)], axis=1)
    full = full.reshape(ny, nz, rows, tok)

    partial_grad = weight_gradient(full, cots)
    weight_grad = lax.psum_scatter(partial_grad, "z", scatter_dimension=0, tiled=False)
    weight_grad = weight_grad.astype(jnp.float32)
    weights = after(weights, partial_grad)
    part, dx = products(full, weights, cots)
    dx = sum_cores(dx.reshape(2, ny, -1, tok))
    part = after(part, dx)
    part = [lax.dynamic_index_in_dim(part, (x - y - d) % ny, 0, keepdims=False) for d in range(ny)]
    queries = total(exchange(part, "y"))
    token_grad = scatter_plane(dx).T
    return (queries, token_grad, weight_grad)


def solution(mesh):
    cube = Mesh(mesh.devices.reshape(4, 8, 4, 2), ("y", "z", "x", "core"))
    spec = P(("y", "z"), ("x", "core"))
    return jax.shard_map(
        local, mesh=cube, in_specs=(spec,) * 4, out_specs=(spec,) * 3, check_vma=False
    )
```

```python
import functools

import jax
import jax.numpy as jnp
from jax import lax
from jax.experimental import pallas as pl
from jax.experimental.pallas import tpu as pltpu
from jax.sharding import Mesh, PartitionSpec as P

BR = 32
BC = 128
TOP = 2.0
STEP = 2


def shift(a, axis, step):
    n = lax.axis_size(axis)
    return lax.ppermute(a, axis, [(i, (i + step) % n) for i in range(n)])


def together(*arrays):
    return lax.optimization_barrier(arrays)


def after(a, *others):
    return lax.optimization_barrier((a,) + others)[0]


def scale_kernel(v_ref, s_ref, o_ref):
    rows, width = v_ref.shape
    for i in range(0, rows, BR):
        for j in range(0, width, BC):
            scale = s_ref[i // BR : i // BR + 1, j // BC : j // BC + 1].astype(jnp.float32)
            value = v_ref[i : i + BR, j : j + BC].astype(jnp.float32)
            o_ref[i : i + BR, j : j + BC] = (value * scale).astype(o_ref.dtype)


def widen_kernel(a_ref, o_ref):
    o_ref[...] = a_ref[...].astype(o_ref.dtype)


def grad_kernel(core_ref, mine_ref, other_ref, d_ref, o_ref, acc, p_ref):
    @pl.when(pl.program_id(0) == 0)
    def _():
        acc[...] = jnp.zeros_like(acc)

    half, rows, width = o_ref.shape[0] // 2, *o_ref.shape[1:]
    nb = rows // BR
    for k in range(2 * half):
        x = (mine_ref if k < half else other_ref)[0, k % half]
        p_ref[k] = jnp.dot(x, d_ref[0], preferred_element_type=jnp.float32)
        p = p_ref[k].reshape(nb, BR, width)
        col = jnp.sum(p * p, axis=1)
        tot = jnp.concatenate(
            [
                jnp.broadcast_to(jnp.sum(col[:, j : j + BC], axis=1, keepdims=True), (nb, BC))
                for j in range(0, width, BC)
            ],
            axis=1,
        )
        scale = jnp.sqrt(tot * 2.0**-24 + 1e-6).astype(jnp.bfloat16).astype(jnp.float32)
        inv = 0.015625 / scale
        for i in range(nb):
            part = p_ref[k, i * BR : (i + 1) * BR, :]
            level = jnp.clip(part * inv[i : i + 1, :], -TOP, TOP).astype(jnp.bfloat16)
            acc[k, i * BR : (i + 1) * BR, :] += level.astype(jnp.float32) * scale[i : i + 1, :]

    @pl.when(pl.program_id(0) == pl.num_programs(0) - 1)
    def _():
        for r in range(2):
            at = lax.rem(core_ref[0] + r, 2) * half
            o_ref[pl.ds(at, half)] = acc[r * half : (r + 1) * half].astype(o_ref.dtype)


def weight_gradient(core, mine, other, cots):
    groups, half, rows, tok = mine.shape
    cols = cots.shape[2]
    whole = (2 * half, rows, cols)
    return pl.pallas_call(
        grad_kernel,
        grid_spec=pltpu.PrefetchScalarGridSpec(
            num_scalar_prefetch=1,
            grid=(groups,),
            in_specs=[
                pl.BlockSpec((1, half, rows, tok), lambda g, c: (g, 0, 0, 0)),
                pl.BlockSpec((1, half, rows, tok), lambda g, c: (g, 0, 0, 0)),
                pl.BlockSpec((1, tok, cols), lambda g, c: (g, 0, 0)),
            ],
            out_specs=pl.BlockSpec(whole, lambda g, c: (0, 0, 0)),
            scratch_shapes=[pltpu.VMEM(whole, jnp.float32)] * 2,
        ),
        out_shape=jax.ShapeDtypeStruct(whole, jnp.bfloat16),
        compiler_params=pltpu.CompilerParams(vmem_limit_bytes=48 * 2**20),
        cost_estimate=pl.CostEstimate(
            flops=16 * 2 * groups * half * rows * tok * cols, bytes_accessed=2**23, transcendentals=0
        ),
    )(core, mine, other, cots)


def terms_kernel(core_ref, w_ref, d_ref, dx_ref):
    n, rows, width = w_ref.shape
    ny, tok = d_ref.shape[:2]
    terms = lax.dot_general(
        w_ref[...].reshape(n * rows, width),
        d_ref[...].reshape(ny * tok, width),
        (((1,), (1,)), ((), ())),
        preferred_element_type=jnp.float32,
    ).astype(jnp.bfloat16)
    for k in range(ny):
        dx_ref[0, k] = terms[:, k * tok : (k + 1) * tok].reshape(n, rows, tok)


def query_kernel(core_ref, mine_ref, other_ref, w_ref, q_ref, acc):
    i = pl.program_id(0)
    n, rows, width = w_ref.shape
    ny, half, _, tok = mine_ref.shape
    steps = half // n

    @pl.when(i == 0)
    def _():
        acc[...] = jnp.zeros_like(acc)

    w = w_ref[...].reshape(n * rows, width)

    def add(x_ref, at):
        for k in range(ny):
            x = x_ref[k, at : at + n].reshape(n * rows, tok)
            acc[k] += lax.dot_general(
                x, w, (((0,), (0,)), ((), ())), preferred_element_type=jnp.float32
            )

    for s in range(2 * steps):
        pl.when(i == s)(functools.partial(add, mine_ref if s < steps else other_ref, s % steps * n))

    @pl.when(i == 2 * steps - 1)
    def _():
        q_ref[...] = acc[...].astype(q_ref.dtype)


def weight_blocks(rows, width, steps):
    return pl.BlockSpec(
        (STEP, rows, width), lambda i, c: (lax.rem(c[0] + i // steps, 2) * steps + i % steps, 0, 0)
    )


def gradient_terms(core, weights, cots):
    nz, rows, width = weights.shape
    ny, tok = cots.shape[:2]
    steps = nz // STEP // 2
    return pl.pallas_call(
        terms_kernel,
        grid_spec=pltpu.PrefetchScalarGridSpec(
            num_scalar_prefetch=1,
            grid=(2 * steps,),
            in_specs=[
                weight_blocks(rows, width, steps),
                pl.BlockSpec((ny, tok, width), lambda i, c: (0, 0, 0)),
            ],
            out_specs=pl.BlockSpec(
                (1, ny, STEP, rows, tok), lambda i, c: (i // steps, 0, i % steps, 0, 0)
            ),
        ),
        out_shape=jax.ShapeDtypeStruct((2, ny, nz // 2, rows, tok), jnp.bfloat16),
        compiler_params=pltpu.CompilerParams(vmem_limit_bytes=48 * 2**20),
        cost_estimate=pl.CostEstimate(
            flops=8 * 2 * ny * nz * rows * width * tok, bytes_accessed=2**22, transcendentals=0
        ),
    )(core, weights, cots)


def query_parts(core, mine, other, weights):
    nz, rows, width = weights.shape
    ny, half, _, tok = mine.shape
    steps = half // STEP
    tokens = pl.BlockSpec((ny, half, rows, tok), lambda i, c: (0, 0, 0, 0))
    return pl.pallas_call(
        query_kernel,
        grid_spec=pltpu.PrefetchScalarGridSpec(
            num_scalar_prefetch=1,
            grid=(2 * steps,),
            in_specs=[tokens, tokens, weight_blocks(rows, width, steps)],
            out_specs=pl.BlockSpec((ny, tok, width), lambda i, c: (0, 0, 0)),
            scratch_shapes=[pltpu.VMEM((ny, tok, width), jnp.float32)],
        ),
        out_shape=jax.ShapeDtypeStruct((ny, tok, width), jnp.bfloat16),
        compiler_params=pltpu.CompilerParams(vmem_limit_bytes=48 * 2**20),
        cost_estimate=pl.CostEstimate(
            flops=8 * 2 * ny * nz * rows * width * tok, bytes_accessed=2**22, transcendentals=0
        ),
    )(core, mine, other, weights)


def exchange(blocks, axis):
    return [blocks[0]] + [shift(blocks[d], axis, d) for d in range(1, len(blocks))]


def total(parts):
    return sum(p.astype(jnp.float32) for p in parts).astype(jnp.bfloat16)


def around(a, k):
    n = lax.axis_size("x")
    pairs = [(i * n + j, j * n + (i + k) % n) for i in range(n) for j in range(n)]
    return lax.ppermute(a, ("y", "x"), pairs)


def sum_cores(terms):
    return total([terms[0], shift(terms[1], "core", 1)])


def scatter_plane(terms):
    x, y, n = lax.axis_index("x"), lax.axis_index("y"), lax.axis_size("x")
    pick = lambda a, i: lax.dynamic_index_in_dim(a, i % n, 0, keepdims=False)
    rows = jnp.stack(exchange([pick(terms, x - y - d) for d in range(n)], "y"))
    return total(exchange([pick(rows, y - x - d) for d in range(n)], "x"))


def local(tokens, weight_values, weight_scales, out_cotangent):
    x, y = lax.axis_index("x"), lax.axis_index("y")
    core = lax.axis_index("core").astype(jnp.int32).reshape(1)
    ny, nz = lax.axis_size("y"), lax.axis_size("z")
    rows, width = weight_values.shape
    tok = tokens.shape[0]

    weights = pl.pallas_call(
        scale_kernel, out_shape=jax.ShapeDtypeStruct((rows, width), jnp.bfloat16)
    )(weight_values, weight_scales)
    weights = lax.all_gather(weights, "z", axis=0)
    tokens = tokens.T
    cots = [shift(out_cotangent, "y", -d) for d in range(1, ny)]
    mine = [around(tokens, k) for k in range(2)]
    tokens = after(tokens, cots[0])
    mine += [around(tokens, k) for k in range(2, ny)]
    *mine, c1, c2, c3 = together(*mine, *cots)
    cots = jnp.stack([out_cotangent, c1, c2, c3])
    cots = jnp.stack([lax.dynamic_index_in_dim(cots, (x - k - y) % ny, 0, keepdims=False) for k in range(ny)])
    mine = jnp.stack(mine).reshape(ny, nz // 2, rows, tok)
    other = shift(mine, "core", 1)

    partial_grad = weight_gradient(core, mine, other, cots)
    weight_grad = lax.psum_scatter(partial_grad, "z", scatter_dimension=0, tiled=False)
    weight_grad = pl.pallas_call(
        widen_kernel, out_shape=jax.ShapeDtypeStruct((rows, width), jnp.float32)
    )(weight_grad)
    weights = after(weights, partial_grad)
    dx = gradient_terms(core, weights, cots)
    part = query_parts(core, mine, other, after(weights, dx))
    dx = sum_cores(dx.reshape(2, ny, -1, tok))
    part = after(part, dx)
    part = [lax.dynamic_index_in_dim(part, (x - y - d) % ny, 0, keepdims=False) for d in range(ny)]
    queries = total(exchange(part, "y"))
    token_grad = scatter_plane(dx).T
    return (queries, token_grad, weight_grad)


def solution(mesh):
    cube = Mesh(mesh.devices.reshape(4, 8, 4, 2), ("y", "z", "x", "core"))
    spec = P(("y", "z"), ("x", "core"))
    return jax.shard_map(
        local, mesh=cube, in_specs=(spec,) * 4, out_specs=(spec,) * 3, check_vma=False
    )
```

```python
import functools

import jax
import jax.numpy as jnp
from jax import lax
from jax.experimental import pallas as pl
from jax.experimental.pallas import tpu as pltpu
from jax.sharding import Mesh, PartitionSpec as P

BR = 32
BC = 128
TOP = 2.0
REST = 128
STEP = 2


def shift(a, axis, step):
    n = lax.axis_size(axis)
    return lax.ppermute(a, axis, [(i, (i + step) % n) for i in range(n)])


def together(*arrays):
    return lax.optimization_barrier(arrays)


def after(a, *others):
    return lax.optimization_barrier((a,) + others)[0]


def scale_kernel(v_ref, s_ref, o_ref):
    rows, width = v_ref.shape
    for i in range(0, rows, BR):
        for j in range(0, width, BC):
            scale = s_ref[i // BR : i // BR + 1, j // BC : j // BC + 1].astype(jnp.float32)
            value = v_ref[i : i + BR, j : j + BC].astype(jnp.float32)
            o_ref[i : i + BR, j : j + BC] = (value * scale).astype(o_ref.dtype)


def finish_kernel(a_ref, parts_ref, o_ref):
    cut = a_ref.shape[1]
    o_ref[:, :cut] = a_ref[...].astype(jnp.float32)
    o_ref[:, cut:] = jnp.sum(parts_ref[...].astype(jnp.float32), axis=0)


def grad_kernel(core_ref, mine_ref, other_ref, d_ref, o_ref, rest_ref, acc, p_ref):
    @pl.when(pl.program_id(0) == 0)
    def _():
        acc[...] = jnp.zeros_like(acc)

    half, rows, width = acc.shape[0] // 2, *acc.shape[1:]
    nb = rows // BR
    for k in range(2 * half):
        x = (mine_ref if k < half else other_ref)[0, k % half]
        p_ref[k] = jnp.dot(x, d_ref[0], preferred_element_type=jnp.float32)
        p = p_ref[k].reshape(nb, BR, width)
        col = jnp.sum(p * p, axis=1)
        tot = jnp.concatenate(
            [
                jnp.broadcast_to(jnp.sum(col[:, j : j + BC], axis=1, keepdims=True), (nb, BC))
                for j in range(0, width, BC)
            ],
            axis=1,
        )
        scale = jnp.sqrt(tot * 2.0**-24 + 1e-6).astype(jnp.bfloat16).astype(jnp.float32)
        inv = 0.015625 / scale
        for i in range(nb):
            part = p_ref[k, i * BR : (i + 1) * BR, :]
            level = jnp.clip(part * inv[i : i + 1, :], -TOP, TOP).astype(jnp.bfloat16)
            acc[k, i * BR : (i + 1) * BR, :] += level.astype(jnp.float32) * scale[i : i + 1, :]

    @pl.when(pl.program_id(0) == pl.num_programs(0) - 1)
    def _():
        for r in range(2):
            at = lax.rem(core_ref[0] + r, 2) * half
            done = acc[r * half : (r + 1) * half].astype(o_ref.dtype)
            cut = o_ref.shape[2]
            o_ref[pl.ds(at, half)] = done[:, :, :cut]
            rest_ref[pl.ds(at, half)] = done[:, :, cut:]


def weight_gradient(core, mine, other, cots):
    groups, half, rows, tok = mine.shape
    cols = cots.shape[2]
    whole = (2 * half, rows, cols)
    shapes = [(2 * half, rows, cols - REST), (2 * half, rows, REST)]
    return pl.pallas_call(
        grad_kernel,
        grid_spec=pltpu.PrefetchScalarGridSpec(
            num_scalar_prefetch=1,
            grid=(groups,),
            in_specs=[
                pl.BlockSpec((1, half, rows, tok), lambda g, c: (g, 0, 0, 0)),
                pl.BlockSpec((1, half, rows, tok), lambda g, c: (g, 0, 0, 0)),
                pl.BlockSpec((1, tok, cols), lambda g, c: (g, 0, 0)),
            ],
            out_specs=[pl.BlockSpec(s, lambda g, c: (0, 0, 0)) for s in shapes],
            scratch_shapes=[pltpu.VMEM(whole, jnp.float32)] * 2,
        ),
        out_shape=[jax.ShapeDtypeStruct(s, jnp.bfloat16) for s in shapes],
        compiler_params=pltpu.CompilerParams(vmem_limit_bytes=48 * 2**20),
        cost_estimate=pl.CostEstimate(
            flops=16 * 2 * groups * half * rows * tok * cols, bytes_accessed=2**23, transcendentals=0
        ),
    )(core, mine, other, cots)


def terms_kernel(core_ref, w_ref, d_ref, dx_ref):
    n, rows, width = w_ref.shape
    ny, tok = d_ref.shape[:2]
    terms = lax.dot_general(
        w_ref[...].reshape(n * rows, width),
        d_ref[...].reshape(ny * tok, width),
        (((1,), (1,)), ((), ())),
        preferred_element_type=jnp.float32,
    ).astype(jnp.bfloat16)
    for k in range(ny):
        dx_ref[0, k] = terms[:, k * tok : (k + 1) * tok].reshape(n, rows, tok)


def query_kernel(core_ref, mine_ref, other_ref, w_ref, q_ref, acc):
    i = pl.program_id(0)
    n, rows, width = w_ref.shape
    ny, half, _, tok = mine_ref.shape
    steps = half // n

    @pl.when(i == 0)
    def _():
        acc[...] = jnp.zeros_like(acc)

    w = w_ref[...].reshape(n * rows, width)

    def add(x_ref, at):
        for k in range(ny):
            x = x_ref[k, at : at + n].reshape(n * rows, tok)
            acc[k] += lax.dot_general(
                x, w, (((0,), (0,)), ((), ())), preferred_element_type=jnp.float32
            )

    for s in range(2 * steps):
        pl.when(i == s)(functools.partial(add, mine_ref if s < steps else other_ref, s % steps * n))

    @pl.when(i == 2 * steps - 1)
    def _():
        q_ref[...] = acc[...].astype(q_ref.dtype)


def weight_blocks(rows, width, steps):
    return pl.BlockSpec(
        (STEP, rows, width), lambda i, c: (lax.rem(c[0] + i // steps, 2) * steps + i % steps, 0, 0)
    )


def gradient_terms(core, weights, cots):
    nz, rows, width = weights.shape
    ny, tok = cots.shape[:2]
    steps = nz // STEP // 2
    return pl.pallas_call(
        terms_kernel,
        grid_spec=pltpu.PrefetchScalarGridSpec(
            num_scalar_prefetch=1,
            grid=(2 * steps,),
            in_specs=[
                weight_blocks(rows, width, steps),
                pl.BlockSpec((ny, tok, width), lambda i, c: (0, 0, 0)),
            ],
            out_specs=pl.BlockSpec(
                (1, ny, STEP, rows, tok), lambda i, c: (i // steps, 0, i % steps, 0, 0)
            ),
        ),
        out_shape=jax.ShapeDtypeStruct((2, ny, nz // 2, rows, tok), jnp.bfloat16),
        compiler_params=pltpu.CompilerParams(vmem_limit_bytes=48 * 2**20),
        cost_estimate=pl.CostEstimate(
            flops=8 * 2 * ny * nz * rows * width * tok, bytes_accessed=2**22, transcendentals=0
        ),
    )(core, weights, cots)


def query_parts(core, mine, other, weights):
    nz, rows, width = weights.shape
    ny, half, _, tok = mine.shape
    steps = half // STEP
    tokens = pl.BlockSpec((ny, half, rows, tok), lambda i, c: (0, 0, 0, 0))
    return pl.pallas_call(
        query_kernel,
        grid_spec=pltpu.PrefetchScalarGridSpec(
            num_scalar_prefetch=1,
            grid=(2 * steps,),
            in_specs=[tokens, tokens, weight_blocks(rows, width, steps)],
            out_specs=pl.BlockSpec((ny, tok, width), lambda i, c: (0, 0, 0)),
            scratch_shapes=[pltpu.VMEM((ny, tok, width), jnp.float32)],
        ),
        out_shape=jax.ShapeDtypeStruct((ny, tok, width), jnp.bfloat16),
        compiler_params=pltpu.CompilerParams(vmem_limit_bytes=48 * 2**20),
        cost_estimate=pl.CostEstimate(
            flops=8 * 2 * ny * nz * rows * width * tok, bytes_accessed=2**22, transcendentals=0
        ),
    )(core, mine, other, weights)


def exchange(blocks, axis):
    return [blocks[0]] + [shift(blocks[d], axis, d) for d in range(1, len(blocks))]


def total(parts):
    return sum(p.astype(jnp.float32) for p in parts).astype(jnp.bfloat16)


def around(a, k):
    n = lax.axis_size("x")
    pairs = [(i * n + j, j * n + (i + k) % n) for i in range(n) for j in range(n)]
    return lax.ppermute(a, ("y", "x"), pairs)


def sum_cores(terms):
    return total([terms[0], shift(terms[1], "core", 1)])


def scatter_plane(terms):
    x, y, n = lax.axis_index("x"), lax.axis_index("y"), lax.axis_size("x")
    pick = lambda a, i: lax.dynamic_index_in_dim(a, i % n, 0, keepdims=False)
    rows = jnp.stack(exchange([pick(terms, x - y - d) for d in range(n)], "y"))
    return total(exchange([pick(rows, y - x - d) for d in range(n)], "x"))


def local(tokens, weight_values, weight_scales, out_cotangent):
    x, y = lax.axis_index("x"), lax.axis_index("y")
    core = lax.axis_index("core").astype(jnp.int32).reshape(1)
    ny, nz = lax.axis_size("y"), lax.axis_size("z")
    rows, width = weight_values.shape
    tok = tokens.shape[0]

    weights = pl.pallas_call(
        scale_kernel, out_shape=jax.ShapeDtypeStruct((rows, width), jnp.bfloat16)
    )(weight_values, weight_scales)
    weights = lax.all_gather(weights, "z", axis=0)
    tokens = tokens.T
    cots = [shift(out_cotangent, "y", -d) for d in range(1, ny)]
    mine = [around(tokens, k) for k in range(2)]
    tokens = after(tokens, cots[0])
    mine += [around(tokens, k) for k in range(2, ny)]
    *mine, c1, c2, c3 = together(*mine, *cots)
    cots = jnp.stack([out_cotangent, c1, c2, c3])
    cots = jnp.stack([lax.dynamic_index_in_dim(cots, (x - k - y) % ny, 0, keepdims=False) for k in range(ny)])
    mine = jnp.stack(mine).reshape(ny, nz // 2, rows, tok)
    other = shift(mine, "core", 1)

    partial_grad, rest = weight_gradient(core, mine, other, cots)
    weight_grad = lax.psum_scatter(partial_grad, "z", scatter_dimension=0, tiled=False)
    weight_grad = pl.pallas_call(
        finish_kernel, out_shape=jax.ShapeDtypeStruct((rows, width), jnp.float32)
    )(weight_grad, lax.all_to_all(rest, "z", split_axis=0, concat_axis=0, tiled=True))
    weights = after(weights, partial_grad)
    dx = gradient_terms(core, weights, cots)
    part = query_parts(core, mine, other, after(weights, dx))
    dx = sum_cores(dx.reshape(2, ny, -1, tok))
    part = after(part, dx)
    part = [lax.dynamic_index_in_dim(part, (x - y - d) % ny, 0, keepdims=False) for d in range(ny)]
    queries = total(exchange(part, "y"))
    token_grad = scatter_plane(dx).T
    return (queries, token_grad, weight_grad)


def solution(mesh):
    cube = Mesh(mesh.devices.reshape(4, 8, 4, 2), ("y", "z", "x", "core"))
    spec = P(("y", "z"), ("x", "core"))
    return jax.shard_map(
        local, mesh=cube, in_specs=(spec,) * 4, out_specs=(spec,) * 3, check_vma=False
    )
```

```python
import functools

import jax
import jax.numpy as jnp
from jax import lax
from jax.experimental import pallas as pl
from jax.experimental.pallas import tpu as pltpu
from jax.sharding import Mesh, PartitionSpec as P

BR = 32
BC = 128
TOP = 2.0
STEP = 2


def shift(a, axis, step):
    n = lax.axis_size(axis)
    return lax.ppermute(a, axis, [(i, (i + step) % n) for i in range(n)])


def together(*arrays):
    return lax.optimization_barrier(arrays)


def after(a, *others):
    return lax.optimization_barrier((a,) + others)[0]


def scale_kernel(v_ref, s_ref, o_ref):
    rows, width = v_ref.shape
    for i in range(0, rows, BR):
        for j in range(0, width, BC):
            scale = s_ref[i // BR : i // BR + 1, j // BC : j // BC + 1].astype(jnp.float32)
            value = v_ref[i : i + BR, j : j + BC].astype(jnp.float32)
            o_ref[i : i + BR, j : j + BC] = (value * scale).astype(o_ref.dtype)


def widen_kernel(a_ref, o_ref):
    o_ref[...] = a_ref[...].astype(o_ref.dtype)


def grad_kernel(core_ref, mine_ref, other_ref, d_ref, o_ref, acc, p_ref):
    @pl.when(pl.program_id(0) == 0)
    def _():
        acc[...] = jnp.zeros_like(acc)

    half, rows, width = o_ref.shape[0] // 2, *o_ref.shape[1:]
    nb = rows // BR
    for k in range(2 * half):
        x = (mine_ref if k < half else other_ref)[0, k % half]
        p_ref[k] = jnp.dot(x, d_ref[0], preferred_element_type=jnp.float32)
        p = p_ref[k].reshape(nb, BR, width)
        col = jnp.sum(p * p, axis=1)
        tot = jnp.concatenate(
            [
                jnp.broadcast_to(jnp.sum(col[:, j : j + BC], axis=1, keepdims=True), (nb, BC))
                for j in range(0, width, BC)
            ],
            axis=1,
        )
        scale = jnp.sqrt(tot * 2.0**-24 + 1e-6).astype(jnp.bfloat16).astype(jnp.float32)
        inv = 0.015625 / scale
        for i in range(nb):
            part = p_ref[k, i * BR : (i + 1) * BR, :]
            level = jnp.clip(part * inv[i : i + 1, :], -TOP, TOP).astype(jnp.bfloat16)
            acc[k, i * BR : (i + 1) * BR, :] += level.astype(jnp.float32) * scale[i : i + 1, :]

    @pl.when(pl.program_id(0) == pl.num_programs(0) - 1)
    def _():
        for r in range(2):
            at = lax.rem(core_ref[0] + r, 2) * half
            o_ref[pl.ds(at, half)] = acc[r * half : (r + 1) * half].astype(o_ref.dtype)


def weight_gradient(core, mine, other, cots):
    groups, half, rows, tok = mine.shape
    cols = cots.shape[2]
    whole = (2 * half, rows, cols)
    return pl.pallas_call(
        grad_kernel,
        grid_spec=pltpu.PrefetchScalarGridSpec(
            num_scalar_prefetch=1,
            grid=(groups,),
            in_specs=[
                pl.BlockSpec((1, half, rows, tok), lambda g, c: (g, 0, 0, 0)),
                pl.BlockSpec((1, half, rows, tok), lambda g, c: (g, 0, 0, 0)),
                pl.BlockSpec((1, tok, cols), lambda g, c: (g, 0, 0)),
            ],
            out_specs=pl.BlockSpec(whole, lambda g, c: (0, 0, 0)),
            scratch_shapes=[pltpu.VMEM(whole, jnp.float32)] * 2,
        ),
        out_shape=jax.ShapeDtypeStruct(whole, jnp.bfloat16),
        compiler_params=pltpu.CompilerParams(vmem_limit_bytes=48 * 2**20),
        cost_estimate=pl.CostEstimate(
            flops=16 * 2 * groups * half * rows * tok * cols, bytes_accessed=2**23, transcendentals=0
        ),
    )(core, mine, other, cots)


def terms_kernel(core_ref, w_ref, d_ref, dx_ref):
    n, rows, width = w_ref.shape
    ny, tok = d_ref.shape[:2]
    terms = lax.dot_general(
        w_ref[...].reshape(n * rows, width),
        d_ref[...].reshape(ny * tok, width),
        (((1,), (1,)), ((), ())),
        preferred_element_type=jnp.float32,
    ).astype(jnp.bfloat16)
    for k in range(ny):
        dx_ref[0, k] = terms[:, k * tok : (k + 1) * tok].reshape(n, rows, tok)


def query_kernel(core_ref, mine_ref, other_ref, w_ref, q_ref, acc):
    i = pl.program_id(0)
    n, rows, width = w_ref.shape
    ny, half, _, tok = mine_ref.shape
    steps = half // n

    @pl.when(i == 0)
    def _():
        acc[...] = jnp.zeros_like(acc)

    w = w_ref[...].reshape(n * rows, width)

    def add(x_ref, at):
        for k in range(ny):
            x = x_ref[k, at : at + n].reshape(n * rows, tok)
            acc[k] += lax.dot_general(
                x, w, (((0,), (0,)), ((), ())), preferred_element_type=jnp.float32
            )

    for s in range(2 * steps):
        pl.when(i == s)(functools.partial(add, mine_ref if s < steps else other_ref, s % steps * n))

    @pl.when(i == 2 * steps - 1)
    def _():
        q_ref[...] = acc[...].astype(q_ref.dtype)


def weight_blocks(rows, width, steps):
    return pl.BlockSpec(
        (STEP, rows, width), lambda i, c: (lax.rem(c[0] + i // steps, 2) * steps + i % steps, 0, 0)
    )


def gradient_terms(core, weights, cots):
    nz, rows, width = weights.shape
    ny, tok = cots.shape[:2]
    steps = nz // STEP // 2
    return pl.pallas_call(
        terms_kernel,
        grid_spec=pltpu.PrefetchScalarGridSpec(
            num_scalar_prefetch=1,
            grid=(2 * steps,),
            in_specs=[
                weight_blocks(rows, width, steps),
                pl.BlockSpec((ny, tok, width), lambda i, c: (0, 0, 0)),
            ],
            out_specs=pl.BlockSpec(
                (1, ny, STEP, rows, tok), lambda i, c: (i // steps, 0, i % steps, 0, 0)
            ),
        ),
        out_shape=jax.ShapeDtypeStruct((2, ny, nz // 2, rows, tok), jnp.bfloat16),
        compiler_params=pltpu.CompilerParams(vmem_limit_bytes=48 * 2**20),
        cost_estimate=pl.CostEstimate(
            flops=8 * 2 * ny * nz * rows * width * tok, bytes_accessed=2**22, transcendentals=0
        ),
    )(core, weights, cots)


def query_parts(core, mine, other, weights):
    nz, rows, width = weights.shape
    ny, half, _, tok = mine.shape
    steps = half // STEP
    tokens = pl.BlockSpec((ny, half, rows, tok), lambda i, c: (0, 0, 0, 0))
    return pl.pallas_call(
        query_kernel,
        grid_spec=pltpu.PrefetchScalarGridSpec(
            num_scalar_prefetch=1,
            grid=(2 * steps,),
            in_specs=[tokens, tokens, weight_blocks(rows, width, steps)],
            out_specs=pl.BlockSpec((ny, tok, width), lambda i, c: (0, 0, 0)),
            scratch_shapes=[pltpu.VMEM((ny, tok, width), jnp.float32)],
        ),
        out_shape=jax.ShapeDtypeStruct((ny, tok, width), jnp.bfloat16),
        compiler_params=pltpu.CompilerParams(vmem_limit_bytes=48 * 2**20),
        cost_estimate=pl.CostEstimate(
            flops=8 * 2 * ny * nz * rows * width * tok, bytes_accessed=2**22, transcendentals=0
        ),
    )(core, mine, other, weights)


def exchange(blocks, axis):
    return [blocks[0]] + [shift(blocks[d], axis, d) for d in range(1, len(blocks))]


def total(parts):
    return sum(p.astype(jnp.float32) for p in parts).astype(jnp.bfloat16)


def around(a, k):
    n = lax.axis_size("x")
    pairs = [(i * n + j, j * n + (i + k) % n) for i in range(n) for j in range(n)]
    return lax.ppermute(a, ("y", "x"), pairs)


def sum_cores(terms):
    return total([terms[0], shift(terms[1], "core", 1)])


def scatter_plane(terms):
    x, y, n = lax.axis_index("x"), lax.axis_index("y"), lax.axis_size("x")
    pick = lambda a, i: lax.dynamic_index_in_dim(a, i % n, 0, keepdims=False)
    rows = jnp.stack(exchange([pick(terms, x - y - d) for d in range(n)], "y"))
    return total(exchange([pick(rows, y - x - d) for d in range(n)], "x"))


def local(tokens, weight_values, weight_scales, out_cotangent):
    x, y = lax.axis_index("x"), lax.axis_index("y")
    core = lax.axis_index("core").astype(jnp.int32).reshape(1)
    ny, nz = lax.axis_size("y"), lax.axis_size("z")
    rows, width = weight_values.shape
    tok = tokens.shape[0]

    weights = pl.pallas_call(
        scale_kernel, out_shape=jax.ShapeDtypeStruct((rows, width), jnp.bfloat16)
    )(weight_values, weight_scales)
    weights = lax.all_gather(weights, "z", axis=0)
    tokens = tokens.T
    cots = [shift(out_cotangent, "y", -d) for d in range(1, ny)]
    mine = [around(tokens, k) for k in range(2)]
    tokens = after(tokens, cots[0])
    mine += [around(tokens, k) for k in range(2, ny)]
    *mine, c1, c2, c3 = together(*mine, *cots)
    cots = jnp.stack([out_cotangent, c1, c2, c3])
    cots = jnp.stack([lax.dynamic_index_in_dim(cots, (x - k - y) % ny, 0, keepdims=False) for k in range(ny)])
    mine = jnp.stack(mine).reshape(ny, nz // 2, rows, tok)
    other = shift(mine, "core", 1)

    partial_grad = weight_gradient(core, mine, other, cots)
    weight_grad = lax.psum_scatter(partial_grad, "z", scatter_dimension=0, tiled=False)
    weight_grad = pl.pallas_call(
        widen_kernel,
        grid=(2,),
        in_specs=[pl.BlockSpec((rows // 2, width), lambda i: (i, 0))],
        out_specs=pl.BlockSpec((rows // 2, width), lambda i: (i, 0)),
        out_shape=jax.ShapeDtypeStruct((rows, width), jnp.float32),
    )(weight_grad)
    weights = after(weights, partial_grad)
    dx = gradient_terms(core, weights, cots)
    part = query_parts(core, mine, other, after(weights, dx))
    dx = sum_cores(dx.reshape(2, ny, -1, tok))
    part = after(part, dx)
    part = [lax.dynamic_index_in_dim(part, (x - y - d) % ny, 0, keepdims=False) for d in range(ny)]
    queries = total(exchange(part, "y"))
    token_grad = scatter_plane(dx).T
    return (queries, token_grad, weight_grad)


def solution(mesh):
    cube = Mesh(mesh.devices.reshape(4, 8, 4, 2), ("y", "z", "x", "core"))
    spec = P(("y", "z"), ("x", "core"))
    return jax.shard_map(
        local, mesh=cube, in_specs=(spec,) * 4, out_specs=(spec,) * 3, check_vma=False
    )
```
